256 devices in a mesh: row: 32 (over y, x, core), col: 8 (over z).
Axes of the slice: x: 4, y: 4, z: 8, core: 2. Of those that a mesh axis runs over, the one named last changes fastest.
Arguments:
- tokens: bfloat16 [1024, 7168], P('row', 'col'), may hold values from -6 to 6
- w_in: bfloat16 [7168, 28672], P('col', 'row'), may hold values from -0.0625 to 0.0625
- w_out: bfloat16 [28672, 7168], P('row', 'col'), may hold values from -0.03125 to 0.03125
- grad_out: bfloat16 [1024, 7168], P('row', 'col'), may hold values from -6 to 6
Outputs:
- output: bfloat16 [1024, 7168], P('row', 'col')
- grad_in: bfloat16 [1024, 7168], P('row', 'col')
- grad_w_in: float32 [7168, 28672], P('col', 'row')
- grad_w_out: float32 [28672, 7168], P('row', 'col')
The draws below stay inside these ranges and needn't reach their ends.
All inputs are finite; a program needn't handle non-finite values.
Results may differ from the reference program's by a relative error of at most 0.0049.
Values may be sent and summed in bfloat16 or wider, within the bound.
No kernel may reach another device: no remote copies, remote signals or barrier semaphores. Data moves between devices by JAX's collectives and lax.ppermute only.
A program may use at most 128 MiB of HBM per device.

```python
import jax
import jax.numpy as jnp
from jax import lax

D = 7168
FF = 28672
TOKENS = 1024


def steps_of(own_key, extent, pieces, least, high):
    gain, own = 1.0, jax.random.fold_in(own_key, 6)
    for position, blocks in pieces:
        steps = jnp.exp(jax.random.uniform(jax.random.fold_in(own, position), (blocks,), jnp.float32, least / len(pieces), high / len(pieces)))
        gain = gain * jnp.repeat(steps, extent[position] // blocks).reshape([-1 if axis == position else 1 for axis in range(len(extent))])
    return gain


def centred(stream_key, shape, spread, limit, shards=(), kind=jnp.bfloat16):
    drawn = spread * jax.random.normal(stream_key, shape, jnp.float32)
    if shards:
        drawn = drawn * steps_of(stream_key, shape, shards, -0.22, 0.18)
    return jnp.clip(drawn, -limit, limit).astype(kind)


def setup_inputs(seed: int = 0) -> dict:
    splits = jax.random.split(jax.random.key(seed), 5)
    tokens = centred(splits[0], (TOKENS, D), 1.0, 6.0, ((0, 32), (1, 8)))
    w_in = centred(splits[1], (D, FF), D ** -0.5, 0.0625, ((0, 8), (1, 32)))
    w_out = centred(splits[2], (FF, D), FF ** -0.5, 0.03125, ((0, 32), (1, 8)))
    grad_out = centred(splits[3], (TOKENS, D), 1.0, 6.0, ((0, 32), (1, 8)))
    return dict(tokens=tokens, w_in=w_in, w_out=w_out, grad_out=grad_out)


def gelu_tanh(h):
    c = 0.7978845608028654
    return 0.5 * h * (1.0 + jnp.tanh(c * (h + 0.044715 * h * h * h)))


def gelu_slope(h):
    c = 0.7978845608028654
    t = jnp.tanh(c * (h + 0.044715 * h * h * h))
    return 0.5 * (1.0 + t) + 0.5 * h * (1.0 - t * t) * c * (1.0 + 3.0 * 0.044715 * h * h)


def matmul(a, b):
    return jnp.dot(a.astype(jnp.float32), b.astype(jnp.float32), precision=lax.Precision.HIGHEST, preferred_element_type=jnp.float32)


def reference(tokens, w_in, w_out, grad_out):
    factor = jnp.float32(TOKENS) ** -0.5
    pre_act = matmul(tokens, w_in)
    act_full = gelu_tanh(pre_act).astype(jnp.bfloat16)
    output = matmul(act_full, w_out).astype(jnp.bfloat16)
    grad_act = matmul(grad_out, w_out.T)
    grad_pre = (grad_act * gelu_slope(pre_act)).astype(jnp.bfloat16)
    grad_w_out = matmul(act_full.T, grad_out) * factor
    grad_w_in = matmul(tokens.T, grad_pre) * factor
    grad_in = matmul(grad_pre, w_in.T).astype(jnp.bfloat16)
    return output, grad_in, grad_w_in, grad_w_out
```

```python
import functools

import jax
import jax.numpy as jnp
from jax import lax
from jax.experimental import pallas as pl
from jax.experimental.pallas import tpu as pltpu
from jax.sharding import Mesh, PartitionSpec as P

BF = jnp.bfloat16
F32 = jnp.float32
NZ = 8
NP = 4
VMEM = pl.BlockSpec(memory_space=pltpu.VMEM)
ANY = pl.BlockSpec(memory_space=pl.ANY)
HBM = pl.BlockSpec(memory_space=pltpu.HBM)
PARAMS = pltpu.CompilerParams(vmem_limit_bytes=20 * 2**20)
SMALL = pltpu.CompilerParams(vmem_limit_bytes=8 * 2**20)


def shape(rows, cols, dtype=BF):
    return jax.ShapeDtypeStruct((rows, cols), dtype)


def cost(args, flops=0):
    nbytes = sum(a.size * a.dtype.itemsize for a in args)
    return pl.CostEstimate(flops=flops, bytes_accessed=nbytes, transcendentals=0)


def call(kernel, outs, args, after, flops=0):
    n = len(args)

    def body(*refs):
        kernel(*refs[:n], *refs[n + 1:])

    return pl.pallas_call(
        body,
        out_shape=outs,
        in_specs=[VMEM] * n + [ANY],
        out_specs=tuple(VMEM for _ in outs),
        compiler_params=PARAMS,
        cost_estimate=cost(args, flops),
    )(*args, after)


def gate(args, after):
    n = len(args)
    return pl.pallas_call(
        lambda *refs: None,
        out_shape=tuple(jax.ShapeDtypeStruct(a.shape, a.dtype) for a in args),
        in_specs=[VMEM] * n + [ANY],
        out_specs=tuple(VMEM for _ in args),
        compiler_params=SMALL,
        input_output_aliases={i: i for i in range(n)},
    )(*args, after)


def shift(x, axis, size, k):
    return lax.ppermute(x, axis, [(i, (i + k) % size) for i in range(size)])


def tile_kernel(x, out):
    n = x.shape[0]
    for i in range(NP * NP):
        out[i * n:(i + 1) * n, :] = x[...]


def gather_xy(x, after):
    n, k = x.shape
    tiled, = call(tile_kernel, (shape(NP * NP * n, k),), (x,), after)
    return lax.all_to_all(tiled, ("y", "x"), 0, 0, tiled=True)


def dot_dims(transposed):
    return (((1,), (1 if transposed else 0,)), ((), ()))


def first_kernel(transposed, own, other, w, _, part, full, held, sem):
    n = own.shape[0]
    rows = n // 2
    copies = []
    for i in range(4):
        src = own if i < 2 else other
        at = (i % 2) * rows
        x = src[at:at + rows, :]
        full[i * rows:(i + 1) * rows, :] = x
        held[i] = lax.dot_general(x, w[...], dot_dims(transposed), preferred_element_type=F32)
        copy = pltpu.make_async_copy(held.at[i], part.at[i * rows:(i + 1) * rows, :], sem.at[i])
        copy.start()
        copies.append(copy)
    for copy in copies:
        copy.wait()


def first(own, w, transposed, after):
    n, k = own.shape
    other = shift(own, "core", 2, 1)
    rows, cols = 2 * n, w.shape[0 if transposed else 1]
    return pl.pallas_call(
        functools.partial(first_kernel, transposed),
        out_shape=(shape(rows, cols, F32), shape(rows, k)),
        in_specs=[VMEM] * 3 + [ANY],
        out_specs=(HBM, VMEM),
        scratch_shapes=[pltpu.VMEM((4, n // 2, cols), F32), pltpu.SemaphoreType.DMA((4,))],
        compiler_params=PARAMS,
        cost_estimate=cost((own, other, w), 2 * rows * k * cols),
    )(own, other, w, after)


def blocks_call(kernel, part, index, args, outs, after):
    n, k = part.shape[0] // NZ, part.shape[1]
    me, index = index[0], index[1:]
    m = len(index)

    def body(at, part, *refs):
        *refs, held, sem = refs
        copies = [
            pltpu.make_async_copy(part.at[pl.ds(pl.multiple_of(lax.rem(at[0] + index[j] + NZ, NZ) * n, n), n), :], held.at[j], sem.at[j])
            for j in range(m)
        ]
        for copy in copies:
            copy.start()
        for copy in copies:
            copy.wait()
        kernel(*[held.at[j] for j in range(m)], *refs[:len(args)], *refs[len(args) + 1:])

    return pl.pallas_call(
        body,
        out_shape=outs,
        in_specs=[pl.BlockSpec(memory_space=pltpu.SMEM), HBM] + [VMEM] * len(args) + [ANY],
        out_specs=tuple(VMEM for _ in outs),
        scratch_shapes=[pltpu.VMEM((m, n, k), F32), pltpu.SemaphoreType.DMA((m,))],
        compiler_params=SMALL,
        cost_estimate=cost(args),
    )(me, part, *args, after)


def start_kernel(*refs):
    m = len(refs) // 2
    for own, out in zip(refs[:m], refs[m:]):
        out[...] = own[...].astype(BF)


def add_kernel(*refs):
    m = len(refs) // 3
    for own, got, out in zip(refs[:m], refs[m:2 * m], refs[2 * m:]):
        out[...] = (own[...] + got[...].astype(F32)).astype(BF)


def act_kernel(own, up, down, act, slope):
    h = own[...] + up[...].astype(F32) + down[...].astype(F32)
    c = 0.7978845608028654
    t = jnp.tanh(c * (h + 0.044715 * h * h * h))
    act[...] = (0.5 * h * (1.0 + t)).astype(BF)
    slope[...] = 0.5 * (1.0 + t) + 0.5 * h * (1.0 - t * t) * c * (1.0 + 3.0 * 0.044715 * h * h)


def pre_kernel(own, up, down, slope, out):
    g = own[...] + up[...].astype(F32) + down[...].astype(F32)
    out[...] = (g * slope[...]).astype(BF)


class Reduce:
    def __init__(self, part, me, hops):
        self.part, self.me, self.hops, self.at = part, me, hops, 0
        self.got = [None, None]

    def step(self, after):
        dirs = [d for d in (0, 1) if self.hops[d] > self.at]
        dist = [self.hops[d] - self.at for d in dirs]
        index = [self.me] + [s if d == 0 else -s for d, s in zip(dirs, dist)]
        n, k = self.part.shape[0] // NZ, self.part.shape[1]
        outs = tuple(shape(n, k) for _ in dirs)
        kernel, args = (start_kernel, ()) if self.at == 0 else (add_kernel, [self.got[d] for d in dirs])
        sent = blocks_call(kernel, self.part, index, args, outs, after)
        for d, x in zip(dirs, sent):
            self.got[d] = shift(x, "col", NZ, 1 if d == 0 else -1)
        self.at += 1
        return sent[0]


class Gather:
    def __init__(self, x, hops):
        self.rel, self.hops, self.at = [None] * NZ, hops, 0
        self.rel[0] = x
        self.last = [x, x]

    def step(self, after):
        dirs = [d for d in (0, 1) if self.hops[d] > self.at]
        if self.at > 0:
            held = gate([self.last[d] for d in dirs], after)
            for d, x in zip(dirs, held):
                self.last[d] = x
                self.rel[NZ - self.at if d == 0 else self.at] = x
        token = self.last[dirs[0]]
        self.at += 1
        for d in dirs:
            self.last[d] = shift(self.last[d], "col", NZ, 1 if d == 0 else -1)
            self.rel[NZ - self.at if d == 0 else self.at] = self.last[d]
        return token


def second_kernel(transposed, me, *refs):
    chunks, (w, _, keep, send, full) = refs[:NZ], refs[NZ:]
    n = chunks[0].shape[0]
    for s in range(NZ):
        start = pl.multiple_of(lax.rem(me[0] + s, NZ) * n, n)
        full[pl.ds(start, n), :] = chunks[s][...]
    h = NZ * n // 2
    d = dot_dims(transposed)
    send[...] = lax.dot_general(full[h:, :], w[...], d, preferred_element_type=F32)
    keep[...] = lax.dot_general(full[:h, :], w[...], d, preferred_element_type=F32)


def second(chunks, w, transposed, me, after):
    n, k = chunks[0].shape
    rows, cols = NZ * n, w.shape[0 if transposed else 1]
    half = shape(rows // 2, cols, F32)
    return pl.pallas_call(
        functools.partial(second_kernel, transposed),
        out_shape=(half, half, shape(rows, k)),
        in_specs=[pl.BlockSpec(memory_space=pltpu.SMEM)] + [VMEM] * (NZ + 1) + [ANY],
        out_specs=(VMEM, VMEM, VMEM),
        compiler_params=PARAMS,
        cost_estimate=cost((*chunks, w), 2 * rows * k * cols),
    )(me, *chunks, w, after)


def pair_kernel(keep, got, out):
    out[...] = (keep[...] + got[...]).astype(BF)


def sum_kernel(x, out):
    n = out.shape[0]
    total = x[0:n, :].astype(F32)
    for i in range(1, NP * NP):
        total += x[i * n:(i + 1) * n, :].astype(F32)
    out[...] = total.astype(BF)


def pair_sum(keep, got, after):
    return call(pair_kernel, (shape(*keep.shape),), (keep, got), after)[0]


def scatter_xy(x):
    return lax.all_to_all(x, ("y", "x"), 0, 0, tiled=True)


def total(x, after):
    return call(sum_kernel, (shape(x.shape[0] // (NP * NP), x.shape[1]),), (x,), after)[0]


def t_mm(a, b):
    return lax.dot_general(a, b, (((0,), (0,)), ((), ())), preferred_element_type=F32)


def per_device(tokens, w_in, w_out, grad_out):
    me = lax.axis_index("col")
    me1 = me[None].astype(jnp.int32)
    factor = float(tokens.shape[0] * 2 * NP * NP) ** (-0.5)

    tok_own = gather_xy(tokens, grad_out)
    gro_own = gather_xy(grad_out, tok_own)
    part, tok = first(tok_own, w_in, False, tokens)
    a = Reduce(part, me1, (4, 3))
    t = a.step(part)
    t = a.step(t)
    gro_own, = gate([gro_own], t)
    gpart, gro = first(gro_own, w_out, True, t)
    b = Reduce(gpart, me1, (3, 4))
    t = a.step(t)
    t = b.step(t)
    t = a.step(t)
    t = b.step(t)
    n, k = part.shape[0] // NZ, part.shape[1]
    act, slope = blocks_call(act_kernel, part, [me1, 0], a.got, (shape(n, k), shape(n, k, F32)), t)
    ga = Gather(act, (4, 3))
    t = ga.step(act)
    t = b.step(t)
    t = ga.step(t)
    t = b.step(t)
    t = ga.step(t)
    gpre, = blocks_call(pre_kernel, gpart, [me1, 0], (*b.got, slope), (shape(n, k),), t)
    gb = Gather(gpre, (3, 4))
    t = gb.step(gpre)
    t = ga.step(t)
    t = gb.step(t)
    keep, send, act_full = second(ga.rel, w_out, False, me1, t)
    t = gb.step(act_full)
    send, = gate([send], t)
    out = pair_sum(keep, shift(send, "core", 2, 1), t)
    t = gb.step(out)
    out = scatter_xy(out)
    keep, send, gpre_full = second(gb.rel, w_in, True, me1, out)
    gin = pair_sum(keep, shift(send, "core", 2, 1), t)
    gin = scatter_xy(gin)
    out = total(out, gpre_full)
    gin = total(gin, out)
    return (out, gin, t_mm(tok, gpre_full) * factor, t_mm(act_full, gro) * factor)


def solution(mesh):
    split = Mesh(mesh.devices.reshape(NP, NP, 2, NZ), ("y", "x", "core", "col"))
    row = ("y", "x", "core")
    in_specs = (P(row, "col"), P("col", row), P(row, "col"), P(row, "col"))
    out_specs = (P(row, "col"), P(row, "col"), P("col", row), P(row, "col"))
    return jax.shard_map(
        per_device, mesh=split, in_specs=in_specs, out_specs=out_specs, check_vma=False
    )
```

```python
import functools

import jax
import jax.numpy as jnp
from jax import lax
from jax.experimental import pallas as pl
from jax.experimental.pallas import tpu as pltpu
from jax.sharding import Mesh, PartitionSpec as P

BF = jnp.bfloat16
F32 = jnp.float32
NZ = 8
NP = 4
VMEM = pl.BlockSpec(memory_space=pltpu.VMEM)
ANY = pl.BlockSpec(memory_space=pl.ANY)
HBM = pl.BlockSpec(memory_space=pltpu.HBM)
PARAMS = pltpu.CompilerParams(vmem_limit_bytes=20 * 2**20)
SMALL = pltpu.CompilerParams(vmem_limit_bytes=8 * 2**20)


def shape(rows, cols, dtype=BF):
    return jax.ShapeDtypeStruct((rows, cols), dtype)


def cost(args, flops=0):
    nbytes = sum(a.size * a.dtype.itemsize for a in args)
    return pl.CostEstimate(flops=flops, bytes_accessed=nbytes, transcendentals=0)


def call(kernel, outs, args, after, flops=0):
    n = len(args)

    def body(*refs):
        kernel(*refs[:n], *refs[n + 1:])

    return pl.pallas_call(
        body,
        out_shape=outs,
        in_specs=[VMEM] * n + [ANY],
        out_specs=tuple(VMEM for _ in outs),
        compiler_params=PARAMS,
        cost_estimate=cost(args, flops),
    )(*args, after)


def gate_kernel(*refs):
    n = len(refs) // 2
    for x, out in zip(refs[:n], refs[n + 1:]):
        out[...] = x[...]


def gate(args, after):
    n = len(args)
    return pl.pallas_call(
        gate_kernel,
        out_shape=tuple(jax.ShapeDtypeStruct(a.shape, a.dtype) for a in args),
        in_specs=[VMEM] * n + [ANY],
        out_specs=tuple(VMEM for _ in args),
        input_output_aliases={i: i for i in range(n)},
        compiler_params=SMALL,
    )(*args, after)


def shift(x, axis, size, k):
    return lax.ppermute(x, axis, [(i, (i + k) % size) for i in range(size)])


def tile_kernel(x, out):
    n = x.shape[0]
    for i in range(NP * NP):
        out[i * n:(i + 1) * n, :] = x[...]


def gather_xy(x, after):
    n, k = x.shape
    tiled, = call(tile_kernel, (shape(NP * NP * n, k),), (x,), after)
    return lax.all_to_all(tiled, ("y", "x"), 0, 0, tiled=True)


def dot_dims(transposed):
    return (((1,), (1 if transposed else 0,)), ((), ()))


def first_kernel(transposed, own, other, w, part, full):
    n = own.shape[0]
    for i, x in enumerate((own, other)):
        full[i * n:(i + 1) * n, :] = x[...]
        part[i * n:(i + 1) * n, :] = lax.dot_general(x[...], w[...], dot_dims(transposed), preferred_element_type=F32)


def first(own, w, transposed, after):
    n, k = own.shape
    other = shift(own, "core", 2, 1)
    rows, cols = 2 * n, w.shape[0 if transposed else 1]
    return call(
        functools.partial(first_kernel, transposed),
        (shape(rows, cols, F32), shape(rows, k)),
        (own, other, w), after, flops=2 * rows * k * cols,
    )


def blocks_call(kernel, part, index, args, outs, after):
    n, k = part.shape[0] // NZ, part.shape[1]
    me, index = index[0], index[1:]
    m = len(index)

    def body(at, part, *refs):
        *refs, held, sem = refs
        copies = [
            pltpu.make_async_copy(part.at[pl.ds(pl.multiple_of(lax.rem(at[0] + index[j] + NZ, NZ) * n, n), n), :], held.at[j], sem.at[j])
            for j in range(m)
        ]
        for copy in copies:
            copy.start()
        for copy in copies:
            copy.wait()
        kernel(*[held.at[j] for j in range(m)], *refs[:len(args)], *refs[len(args) + 1:])

    return pl.pallas_call(
        body,
        out_shape=outs,
        in_specs=[pl.BlockSpec(memory_space=pltpu.SMEM), HBM] + [VMEM] * len(args) + [ANY],
        out_specs=tuple(VMEM for _ in outs),
        scratch_shapes=[pltpu.VMEM((m, n, k), F32), pltpu.SemaphoreType.DMA((m,))],
        compiler_params=SMALL,
        cost_estimate=cost(args),
    )(me, part, *args, after)


def start_kernel(*refs):
    m = len(refs) // 2
    for own, out in zip(refs[:m], refs[m:]):
        out[...] = own[...].astype(BF)


def add_kernel(*refs):
    m = len(refs) // 3
    for own, got, out in zip(refs[:m], refs[m:2 * m], refs[2 * m:]):
        out[...] = (own[...] + got[...].astype(F32)).astype(BF)


def act_kernel(own, up, down, act, slope):
    h = own[...] + up[...].astype(F32) + down[...].astype(F32)
    c = 0.7978845608028654
    t = jnp.tanh(c * (h + 0.044715 * h * h * h))
    act[...] = (0.5 * h * (1.0 + t)).astype(BF)
    slope[...] = 0.5 * (1.0 + t) + 0.5 * h * (1.0 - t * t) * c * (1.0 + 3.0 * 0.044715 * h * h)


def pre_kernel(own, up, down, slope, out):
    g = own[...] + up[...].astype(F32) + down[...].astype(F32)
    out[...] = (g * slope[...]).astype(BF)


class Reduce:
    def __init__(self, part, me, hops):
        self.part, self.me, self.hops, self.at = part, me, hops, 0
        self.got = [None, None]

    def step(self, after):
        dirs = [d for d in (0, 1) if self.hops[d] > self.at]
        dist = [self.hops[d] - self.at for d in dirs]
        index = [self.me] + [s if d == 0 else -s for d, s in zip(dirs, dist)]
        n, k = self.part.shape[0] // NZ, self.part.shape[1]
        outs = tuple(shape(n, k) for _ in dirs)
        kernel, args = (start_kernel, ()) if self.at == 0 else (add_kernel, [self.got[d] for d in dirs])
        sent = blocks_call(kernel, self.part, index, args, outs, after)
        for d, x in zip(dirs, sent):
            self.got[d] = shift(x, "col", NZ, 1 if d == 0 else -1)
        self.at += 1
        return sent[0]


class Gather:
    def __init__(self, x, hops):
        self.rel, self.hops, self.at = [None] * NZ, hops, 0
        self.rel[0] = x
        self.last = [x, x]

    def step(self, after):
        dirs = [d for d in (0, 1) if self.hops[d] > self.at]
        if self.at > 0:
            held = gate([self.last[d] for d in dirs], after)
            for d, x in zip(dirs, held):
                self.last[d] = x
                self.rel[NZ - self.at if d == 0 else self.at] = x
        token = self.last[dirs[0]]
        self.at += 1
        for d in dirs:
            self.last[d] = shift(self.last[d], "col", NZ, 1 if d == 0 else -1)
            self.rel[NZ - self.at if d == 0 else self.at] = self.last[d]
        return token


def second_kernel(transposed, me, *refs):
    chunks, (w, _, keep, send, full) = refs[:NZ], refs[NZ:]
    n = chunks[0].shape[0]
    for s in range(NZ):
        start = pl.multiple_of(lax.rem(me[0] + s, NZ) * n, n)
        full[pl.ds(start, n), :] = chunks[s][...]
    h = NZ * n // 2
    d = dot_dims(transposed)
    send[...] = lax.dot_general(full[h:, :], w[...], d, preferred_element_type=F32)
    keep[...] = lax.dot_general(full[:h, :], w[...], d, preferred_element_type=F32)


def second(chunks, w, transposed, me, after):
    n, k = chunks[0].shape
    rows, cols = NZ * n, w.shape[0 if transposed else 1]
    half = shape(rows // 2, cols, F32)
    return pl.pallas_call(
        functools.partial(second_kernel, transposed),
        out_shape=(half, half, shape(rows, k)),
        in_specs=[pl.BlockSpec(memory_space=pltpu.SMEM)] + [VMEM] * (NZ + 1) + [ANY],
        out_specs=(VMEM, VMEM, VMEM),
        compiler_params=PARAMS,
        cost_estimate=cost((*chunks, w), 2 * rows * k * cols),
    )(me, *chunks, w, after)


def pair_kernel(keep, got, out):
    out[...] = (keep[...] + got[...]).astype(BF)


def sum_kernel(x, out):
    n = out.shape[0]
    total = x[0:n, :].astype(F32)
    for i in range(1, NP * NP):
        total += x[i * n:(i + 1) * n, :].astype(F32)
    out[...] = total.astype(BF)


def pair_sum(keep, got, after):
    return call(pair_kernel, (shape(*keep.shape),), (keep, got), after)[0]


def split_kernel(axis, at, total, mine, sends):
    n = mine.shape[0]
    for d in range(NP):
        rows = total[pl.ds(pl.multiple_of(lax.rem(at[axis] + d, NP) * n, n), n), :]
        if d == 0:
            mine[...] = rows
        else:
            sends[d - 1][...] = rows.astype(BF)


def to_y_kernel(at, keep, got, _, mine, *refs):
    *sends, total = refs
    total[...] = keep[...] + got[...]
    split_kernel(0, at, total, mine, sends)


def to_x_kernel(at, own, r1, r2, r3, _, mine, *refs):
    *sends, total = refs
    total[...] = own[...] + r1[...].astype(F32) + r2[...].astype(F32) + r3[...].astype(F32)
    split_kernel(1, at, total, mine, sends)


def last_kernel(own, r1, r2, r3, out):
    out[...] = (own[...] + r1[...].astype(F32) + r2[...].astype(F32) + r3[...].astype(F32)).astype(BF)


def hand_out(kernel, axis, at, args, after):
    rows, k = args[0].shape
    n = rows // NP
    mine, *sends = pl.pallas_call(
        kernel,
        out_shape=(shape(n, k, F32),) + (shape(n, k),) * (NP - 1),
        in_specs=[pl.BlockSpec(memory_space=pltpu.SMEM)] + [VMEM] * len(args) + [ANY],
        out_specs=(VMEM,) * NP,
        scratch_shapes=[pltpu.VMEM((rows, k), F32)],
        compiler_params=SMALL if rows < 512 else PARAMS,
        cost_estimate=cost(args),
    )(at, *args, after)
    return [mine] + [shift(x, axis, NP, d + 1) for d, x in enumerate(sends)]


def scatter_xy(x):
    return lax.all_to_all(x, ("y", "x"), 0, 0, tiled=True)


def total(x, after):
    return call(sum_kernel, (shape(x.shape[0] // (NP * NP), x.shape[1]),), (x,), after)[0]


def t_mm(a, b):
    return lax.dot_general(a, b, (((0,), (0,)), ((), ())), preferred_element_type=F32)


def per_device(tokens, w_in, w_out, grad_out):
    me = lax.axis_index("col")
    me1 = me[None].astype(jnp.int32)
    at = jnp.stack([lax.axis_index("y"), lax.axis_index("x")]).astype(jnp.int32)
    factor = float(tokens.shape[0] * 2 * NP * NP) ** (-0.5)

    tok_own = gather_xy(tokens, grad_out)
    gro_own = gather_xy(grad_out, tok_own)
    part, tok = first(tok_own, w_in, False, tokens)
    a = Reduce(part, me1, (4, 3))
    t = a.step(part)
    t = a.step(t)
    gro_own, = gate([gro_own], t)
    gpart, gro = first(gro_own, w_out, True, t)
    b = Reduce(gpart, me1, (3, 4))
    t = b.step(gpart)
    t = a.step(t)
    t = b.step(t)
    t = a.step(t)
    t = b.step(t)
    n, k = part.shape[0] // NZ, part.shape[1]
    act, slope = blocks_call(act_kernel, part, [me1, 0], a.got, (shape(n, k), shape(n, k, F32)), t)
    ga = Gather(act, (4, 3))
    t = ga.step(act)
    t = b.step(t)
    t = ga.step(t)
    gpre, = blocks_call(pre_kernel, gpart, [me1, 0], (*b.got, slope), (shape(n, k),), t)
    gb = Gather(gpre, (3, 4))
    t = gb.step(gpre)
    t = ga.step(t)
    t = gb.step(t)
    t = ga.step(t)
    t = gb.step(t)
    keep, send, act_full = second(ga.rel, w_out, False, me1, t)
    got = shift(send, "core", 2, 1)
    t = gb.step(act_full)
    okeep = keep
    keep, send, gpre_full = second(gb.rel, w_in, True, me1, t)
    blocks = hand_out(to_y_kernel, "y", at, (okeep, got), gpre_full)
    gin = pair_sum(keep, shift(send, "core", 2, 1), blocks[0])
    blocks = hand_out(to_x_kernel, "x", at, blocks, gin)
    gin = scatter_xy(gin)
    out, = call(last_kernel, (shape(*blocks[0].shape),), blocks, gpre_full)
    gin = total(gin, gpre_full)
    return (out, gin, t_mm(tok, gpre_full) * factor, t_mm(act_full, gro) * factor)


def solution(mesh):
    split = Mesh(mesh.devices.reshape(NP, NP, 2, NZ), ("y", "x", "core", "col"))
    row = ("y", "x", "core")
    in_specs = (P(row, "col"), P("col", row), P(row, "col"), P(row, "col"))
    out_specs = (P(row, "col"), P(row, "col"), P("col", row), P(row, "col"))
    return jax.shard_map(
        per_device, mesh=split, in_specs=in_specs, out_specs=out_specs, check_vma=False
    )
```

```python
import functools

import jax
import jax.numpy as jnp
from jax import lax
from jax.experimental import pallas as pl
from jax.experimental.pallas import tpu as pltpu
from jax.sharding import Mesh, PartitionSpec as P

BF = jnp.bfloat16
F32 = jnp.float32
NZ = 8
NP = 4
VMEM = pl.BlockSpec(memory_space=pltpu.VMEM)
ANY = pl.BlockSpec(memory_space=pl.ANY)
HBM = pl.BlockSpec(memory_space=pltpu.HBM)
PARAMS = pltpu.CompilerParams(vmem_limit_bytes=20 * 2**20)
SMALL = pltpu.CompilerParams(vmem_limit_bytes=8 * 2**20)


def shape(rows, cols, dtype=BF):
    return jax.ShapeDtypeStruct((rows, cols), dtype)


def cost(args, flops=0):
    nbytes = sum(a.size * a.dtype.itemsize for a in args)
    return pl.CostEstimate(flops=flops, bytes_accessed=nbytes, transcendentals=0)


def call(kernel, outs, args, after, flops=0):
    n = len(args)

    def body(*refs):
        kernel(*refs[:n], *refs[n + 1:])

    return pl.pallas_call(
        body,
        out_shape=outs,
        in_specs=[VMEM] * n + [ANY],
        out_specs=tuple(VMEM for _ in outs),
        compiler_params=PARAMS,
        cost_estimate=cost(args, flops),
    )(*args, after)


def gate_kernel(*refs):
    n = len(refs) // 2
    for x, out in zip(refs[:n], refs[n + 1:]):
        out[...] = x[...]


def gate(args, after):
    n = len(args)
    return pl.pallas_call(
        gate_kernel,
        out_shape=tuple(jax.ShapeDtypeStruct(a.shape, a.dtype) for a in args),
        in_specs=[VMEM] * n + [ANY],
        out_specs=tuple(VMEM for _ in args),
        input_output_aliases={i: i for i in range(n)},
        compiler_params=SMALL,
    )(*args, after)


def shift(x, axis, size, k):
    return lax.ppermute(x, axis, [(i, (i + k) % size) for i in range(size)])


def tile_kernel(x, out):
    n = x.shape[0]
    for i in range(NP * NP):
        out[i * n:(i + 1) * n, :] = x[...]


def gather_xy(x, after):
    n, k = x.shape
    tiled, = call(tile_kernel, (shape(NP * NP * n, k),), (x,), after)
    return lax.all_to_all(tiled, ("y", "x"), 0, 0, tiled=True)


def dot_dims(transposed):
    return (((1,), (1 if transposed else 0,)), ((), ()))


def first_kernel(transposed, own, other, w, part, full):
    n = own.shape[0]
    for i, x in enumerate((own, other)):
        full[i * n:(i + 1) * n, :] = x[...]
        part[i * n:(i + 1) * n, :] = lax.dot_general(x[...], w[...], dot_dims(transposed), preferred_element_type=F32)


def first(own, w, transposed, after):
    n, k = own.shape
    other = shift(own, "core", 2, 1)
    rows, cols = 2 * n, w.shape[0 if transposed else 1]
    return call(
        functools.partial(first_kernel, transposed),
        (shape(rows, cols, F32), shape(rows, k)),
        (own, other, w), after, flops=2 * rows * k * cols,
    )


def blocks_call(kernel, part, index, args, outs, after):
    n, k = part.shape[0] // NZ, part.shape[1]
    me, index = index[0], index[1:]
    m = len(index)

    def body(at, part, *refs):
        *refs, held, sem = refs
        copies = [
            pltpu.make_async_copy(part.at[pl.ds(pl.multiple_of(lax.rem(at[0] + index[j] + NZ, NZ) * n, n), n), :], held.at[j], sem.at[j])
            for j in range(m)
        ]
        for copy in copies:
            copy.start()
        for copy in copies:
            copy.wait()
        kernel(*[held.at[j] for j in range(m)], *refs[:len(args)], *refs[len(args) + 1:])

    return pl.pallas_call(
        body,
        out_shape=outs,
        in_specs=[pl.BlockSpec(memory_space=pltpu.SMEM), HBM] + [VMEM] * len(args) + [ANY],
        out_specs=tuple(VMEM for _ in outs),
        scratch_shapes=[pltpu.VMEM((m, n, k), F32), pltpu.SemaphoreType.DMA((m,))],
        compiler_params=SMALL,
        cost_estimate=cost(args),
    )(me, part, *args, after)


def start_kernel(*refs):
    m = len(refs) // 2
    for own, out in zip(refs[:m], refs[m:]):
        out[...] = own[...].astype(BF)


def add_kernel(*refs):
    m = len(refs) // 3
    for own, got, out in zip(refs[:m], refs[m:2 * m], refs[2 * m:]):
        out[...] = (own[...] + got[...].astype(F32)).astype(BF)


def act_kernel(own, up, down, act, slope):
    h = own[...] + up[...].astype(F32) + down[...].astype(F32)
    c = 0.7978845608028654
    t = jnp.tanh(c * (h + 0.044715 * h * h * h))
    act[...] = (0.5 * h * (1.0 + t)).astype(BF)
    slope[...] = 0.5 * (1.0 + t) + 0.5 * h * (1.0 - t * t) * c * (1.0 + 3.0 * 0.044715 * h * h)


def pre_kernel(own, up, down, slope, out):
    g = own[...] + up[...].astype(F32) + down[...].astype(F32)
    out[...] = (g * slope[...]).astype(BF)


class Reduce:
    def __init__(self, part, me, hops):
        self.part, self.me, self.hops, self.at = part, me, hops, 0
        self.got = [None, None]

    def step(self, after):
        dirs = [d for d in (0, 1) if self.hops[d] > self.at]
        dist = [self.hops[d] - self.at for d in dirs]
        index = [self.me] + [s if d == 0 else -s for d, s in zip(dirs, dist)]
        n, k = self.part.shape[0] // NZ, self.part.shape[1]
        outs = tuple(shape(n, k) for _ in dirs)
        kernel, args = (start_kernel, ()) if self.at == 0 else (add_kernel, [self.got[d] for d in dirs])
        sent = blocks_call(kernel, self.part, index, args, outs, after)
        for d, x in zip(dirs, sent):
            self.got[d] = shift(x, "col", NZ, 1 if d == 0 else -1)
        self.at += 1
        return sent[0]


class Gather:
    def __init__(self, x, hops):
        self.rel, self.hops, self.at = [None] * NZ, hops, 0
        self.rel[0] = x
        self.last = [x, x]

    def step(self, after):
        dirs = [d for d in (0, 1) if self.hops[d] > self.at]
        if self.at > 0:
            held = gate([self.last[d] for d in dirs], after)
            for d, x in zip(dirs, held):
                self.last[d] = x
                self.rel[NZ - self.at if d == 0 else self.at] = x
        token = self.last[dirs[0]]
        self.at += 1
        for d in dirs:
            self.last[d] = shift(self.last[d], "col", NZ, 1 if d == 0 else -1)
            self.rel[NZ - self.at if d == 0 else self.at] = self.last[d]
        return token


def second_kernel(transposed, me, *refs):
    chunks, (w, _, keep, send, full) = refs[:NZ], refs[NZ:]
    n = chunks[0].shape[0]
    for s in range(NZ):
        start = pl.multiple_of(lax.rem(me[0] + s, NZ) * n, n)
        full[pl.ds(start, n), :] = chunks[s][...]
    h = NZ * n // 2
    d = dot_dims(transposed)
    send[...] = lax.dot_general(full[h:, :], w[...], d, preferred_element_type=F32)
    keep[...] = lax.dot_general(full[:h, :], w[...], d, preferred_element_type=F32)


def second(chunks, w, transposed, me, after):
    n, k = chunks[0].shape
    rows, cols = NZ * n, w.shape[0 if transposed else 1]
    half = shape(rows // 2, cols, F32)
    return pl.pallas_call(
        functools.partial(second_kernel, transposed),
        out_shape=(half, half, shape(rows, k)),
        in_specs=[pl.BlockSpec(memory_space=pltpu.SMEM)] + [VMEM] * (NZ + 1) + [ANY],
        out_specs=(VMEM, VMEM, VMEM),
        compiler_params=PARAMS,
        cost_estimate=cost((*chunks, w), 2 * rows * k * cols),
    )(me, *chunks, w, after)


def pair_kernel(keep, got, out):
    out[...] = (keep[...] + got[...]).astype(BF)


def sum_kernel(x, out):
    n = out.shape[0]
    total = x[0:n, :].astype(F32)
    for i in range(1, NP * NP):
        total += x[i * n:(i + 1) * n, :].astype(F32)
    out[...] = total.astype(BF)


def pair_sum(keep, got, after):
    return call(pair_kernel, (shape(*keep.shape),), (keep, got), after)[0]


def split_kernel(axis, at, total, mine, sends):
    n = mine.shape[0]
    for d in range(NP):
        rows = total[pl.ds(pl.multiple_of(lax.rem(at[axis] + d, NP) * n, n), n), :]
        if d == 0:
            mine[...] = rows
        else:
            sends[d - 1][...] = rows.astype(BF)


def to_y_kernel(at, keep, got, _, mine, *refs):
    *sends, total = refs
    total[...] = keep[...] + got[...]
    split_kernel(0, at, total, mine, sends)


def to_x_kernel(at, own, r1, r2, r3, _, mine, *refs):
    *sends, total = refs
    total[...] = own[...] + r1[...].astype(F32) + r2[...].astype(F32) + r3[...].astype(F32)
    split_kernel(1, at, total, mine, sends)


def last_kernel(own, r1, r2, r3, out):
    out[...] = (own[...] + r1[...].astype(F32) + r2[...].astype(F32) + r3[...].astype(F32)).astype(BF)


def hand_out(kernel, axis, at, args, after):
    rows, k = args[0].shape
    n = rows // NP
    mine, *sends = pl.pallas_call(
        kernel,
        out_shape=(shape(n, k, F32),) + (shape(n, k),) * (NP - 1),
        in_specs=[pl.BlockSpec(memory_space=pltpu.SMEM)] + [VMEM] * len(args) + [ANY],
        out_specs=(VMEM,) * NP,
        scratch_shapes=[pltpu.VMEM((rows, k), F32)],
        compiler_params=SMALL if rows < 512 else PARAMS,
        cost_estimate=cost(args),
    )(at, *args, after)
    return [mine] + [shift(x, axis, NP, d + 1) for d, x in enumerate(sends)]


def scatter_xy(x):
    return lax.all_to_all(x, ("y", "x"), 0, 0, tiled=True)


def total(x, after):
    return call(sum_kernel, (shape(x.shape[0] // (NP * NP), x.shape[1]),), (x,), after)[0]


def t_mm(a, b):
    return lax.dot_general(a, b, (((0,), (0,)), ((), ())), preferred_element_type=F32)


def per_device(tokens, w_in, w_out, grad_out):
    me = lax.axis_index("col")
    me1 = me[None].astype(jnp.int32)
    at = jnp.stack([lax.axis_index("y"), lax.axis_index("x")]).astype(jnp.int32)
    factor = float(tokens.shape[0] * 2 * NP * NP) ** (-0.5)

    tok_own = gather_xy(tokens, grad_out)
    gro_own = gather_xy(grad_out, tok_own)
    part, tok = first(tok_own, w_in, False, tokens)
    a = Reduce(part, me1, (4, 3))
    t = a.step(part)
    gro_own, = gate([gro_own], t)
    t = a.step(t)
    gpart, gro = first(gro_own, w_out, True, t)
    b = Reduce(gpart, me1, (3, 4))
    t = b.step(gpart)
    t = a.step(t)
    t = b.step(t)
    t = a.step(t)
    t = b.step(t)
    n, k = part.shape[0] // NZ, part.shape[1]
    act, slope = blocks_call(act_kernel, part, [me1, 0], a.got, (shape(n, k), shape(n, k, F32)), t)
    ga = Gather(act, (4, 3))
    t = ga.step(act)
    t = b.step(t)
    t = ga.step(t)
    gpre, = blocks_call(pre_kernel, gpart, [me1, 0], (*b.got, slope), (shape(n, k),), t)
    gb = Gather(gpre, (3, 4))
    t = gb.step(gpre)
    t = ga.step(t)
    t = gb.step(t)
    t = ga.step(t)
    t = gb.step(t)
    keep, send, act_full = second(ga.rel, w_out, False, me1, t)
    got = shift(send, "core", 2, 1)
    t = gb.step(act_full)
    okeep = keep
    keep, send, gpre_full = second(gb.rel, w_in, True, me1, t)
    blocks = hand_out(to_y_kernel, "y", at, (okeep, got), gpre_full)
    gin = pair_sum(keep, shift(send, "core", 2, 1), blocks[0])
    blocks = hand_out(to_x_kernel, "x", at, blocks, gin)
    gin = scatter_xy(gin)
    out, = call(last_kernel, (shape(*blocks[0].shape),), blocks, gpre_full)
    gin = total(gin, gpre_full)
    return (out, gin, t_mm(tok, gpre_full) * factor, t_mm(act_full, gro) * factor)


def solution(mesh):
    split = Mesh(mesh.devices.reshape(NP, NP, 2, NZ), ("y", "x", "core", "col"))
    row = ("y", "x", "core")
    in_specs = (P(row, "col"), P("col", row), P(row, "col"), P(row, "col"))
    out_specs = (P(row, "col"), P(row, "col"), P("col", row), P(row, "col"))
    return jax.shard_map(
        per_device, mesh=split, in_specs=in_specs, out_specs=out_specs, check_vma=False
    )
```
